32 devices in a mesh: groups: 2 (over y), store: 4 (over x, core), tensor: 4 (over z).
Axes of the slice: x: 2, y: 2, z: 4, core: 2. Of those that a mesh axis runs over, the one named last changes fastest.
Arguments:
- tokens: bfloat16 [2048, 8192], P(('groups', 'store'), 'tensor'), parts along dimension 0, may hold values from -6 to 6
- key_value_weight: bfloat16 [8192, 2048], P('tensor'), may hold values from -0.0625 to 0.0625
- adapter_down_maps: bfloat16 [128, 8192, 128], P(('groups', 'store'), 'tensor'), parts along dimension 0, may hold values from -0.0625 to 0.0625
- adapter_up_maps: bfloat16 [128, 64, 2048], P(('groups', 'store'), 'tensor'), parts along dimension 0, may hold values from -0.75 to 0.75
- local_adapter_ids: int32 [2048], P(('groups', 'store')), parts along dimension 0, may hold values from 0 to 15, as said below
- request_slot_index: int32 [2048], P(('groups', 'store')), parts along dimension 0, may hold values from 0 to 7, as said below
Outputs:
- kv_new: bfloat16 [2048, 2048], P(('groups', 'store'), 'tensor'), parts along dimension 0
The draws below stay inside these ranges and needn't reach their ends.
There are 2 independent parts, one for each index of `groups`. The reference program is written for one: setup_inputs(seed, part) draws one part's arguments, and reference() takes and returns one part's arrays. A program takes and returns all parts, laid end to end along the dimension named above; an argument that names none is the same for every part. Nothing has to cross between parts.
Inputs may be any that keep to these rules, and one draw needn't show every extreme that they name: `local_adapter_ids`: on one device (a block of 256 requests), requests with the same slot have the same local id, and different slots of the same owner hold different local ids. request_slot_index // 2 is the index of store that owns the request's adapter. Among the 256 requests of one device at most 64 have the same owner, and on every device exactly 64 requests have one owner, whose 2 slots are all used.
All inputs are finite; a program needn't handle non-finite values.
Results may differ from the reference program's by a relative error of at most 0.0039.
Values may be sent and summed in bfloat16 or wider, within the bound.
No kernel may reach another device: no remote copies, remote signals or barrier semaphores. Data moves between devices by JAX's collectives and lax.ppermute only.
A program may use at most 128 MiB of HBM per device.

```python
import jax
import jax.numpy as jnp
from jax import lax

MODEL_WIDTH = 8192
KEY_VALUE_WIDTH = 1024
ADAPTER_RANK = 64
SLOTS = 2
REQ_DEV = 256
ADP_DEV = 16
REQUESTS = 1024
ADAPTER_POOL = 64
N_STORE = 4


def plan_requests(key):
    base_key = jax.random.fold_in(key, 11)
    keys = jax.random.split(base_key, 6)
    limit = REQ_DEV // 4
    popular = jax.random.permutation(keys[0], jnp.arange(N_STORE, dtype=jnp.int32))
    rank_of = jnp.argsort(popular, stable=True).astype(jnp.int32)
    forced_owner = jax.random.randint(keys[1], (N_STORE,), 0, N_STORE).astype(jnp.int32)
    candidate = (jnp.arange(N_STORE * limit, dtype=jnp.int32) // limit)[None, :]
    noise = jax.random.randint(keys[2], (N_STORE, N_STORE * limit), 0, N_STORE * 64)
    score = noise + rank_of[candidate] * 48
    score = jnp.where(candidate == forced_owner[:, None], N_STORE * 200, score)
    score = score * (N_STORE * limit) + jnp.arange(N_STORE * limit, dtype=jnp.int32)[None, :]
    order = jnp.argsort(score, axis=1, stable=True).astype(jnp.int32)
    rest = jnp.take_along_axis(jnp.broadcast_to(candidate, score.shape), order[:, :REQ_DEV - limit], axis=1)
    owners = jnp.concatenate([jnp.broadcast_to(forced_owner[:, None], (N_STORE, limit)), rest], axis=1)
    position = jax.random.randint(keys[3], (N_STORE, REQ_DEV), 0, SLOTS)
    request_index = jnp.arange(REQ_DEV, dtype=jnp.int32)[None, :]
    position = jnp.where(request_index < SLOTS, request_index, position)
    shuffle_key = jax.random.randint(keys[4], (N_STORE, REQ_DEV), 0, 4096) * REQ_DEV + request_index
    shuffle = jnp.argsort(shuffle_key, axis=1, stable=True).astype(jnp.int32)
    owners = jnp.take_along_axis(owners, shuffle, axis=1)
    position = jnp.take_along_axis(position, shuffle, axis=1)
    offsets = jax.random.randint(keys[5], (N_STORE, N_STORE), 0, ADP_DEV)
    start = jnp.take_along_axis(offsets, owners, axis=1)
    local_position = (start + position) % ADP_DEV
    slot = owners * SLOTS + position
    return (slot.reshape(-1).astype(jnp.int32), local_position.reshape(-1).astype(jnp.int32))


def draw_local_adapter_ids(key, part):
    shared = plan_requests(key)
    return shared[1]


def draw_request_slot_index(key, part):
    shared = plan_requests(key)
    return shared[0]


def level_of(own_key, dims, cuts, smallest, largest):
    def one(dim, parts):
        steps = jax.random.uniform(jax.random.fold_in(jax.random.fold_in(own_key, 6), dim), (parts,), jnp.float32, smallest / len(cuts), largest / len(cuts))
        return jnp.repeat(jnp.exp(steps), dims[dim] // parts).reshape((-1,) + (1,) * (len(dims) - dim - 1))

    level = one(*cuts[0])
    for cut in cuts[1:]:
        level = level * one(*cut)
    return level


def scatter_about(own_key, dims, deviation, bound, pieces=(), kind=jnp.bfloat16):
    loudness = level_of(own_key, dims, pieces, -0.22, 0.18) if pieces else 1.0
    drawn = jax.random.normal(own_key, dims, jnp.float32) * deviation * loudness
    return jnp.minimum(jnp.maximum(drawn, -bound), bound).astype(kind)


def setup_inputs(seed: int = 0, part: int = 0) -> dict:
    streams_of = jax.random.split(jax.random.key(seed), 7)
    part_splits = jax.random.split(jax.random.fold_in(streams_of[6], part), 7)
    return {
        "tokens": scatter_about(part_splits[0], (REQUESTS, MODEL_WIDTH), 1.0, 6.0, ((0, 4), (1, 4))),
        "key_value_weight": scatter_about(streams_of[1], (MODEL_WIDTH, 2 * KEY_VALUE_WIDTH), MODEL_WIDTH ** -0.5, 0.0625, ((0, 4),)),
        "adapter_down_maps": scatter_about(part_splits[2], (ADAPTER_POOL, MODEL_WIDTH, 2 * ADAPTER_RANK), MODEL_WIDTH ** -0.5, 0.0625, ((0, 4), (1, 4))),
        "adapter_up_maps": scatter_about(part_splits[3], (ADAPTER_POOL, ADAPTER_RANK, 2 * KEY_VALUE_WIDTH), ADAPTER_RANK ** -0.5, 0.75, ((0, 4), (1, 4))),
        "local_adapter_ids": draw_local_adapter_ids(jax.random.fold_in(jax.random.fold_in(streams_of[6], part), 71), part),
        "request_slot_index": draw_request_slot_index(jax.random.fold_in(jax.random.fold_in(streams_of[6], part), 71), part),
    }


def reference(tokens, key_value_weight, adapter_down_maps, adapter_up_maps, local_adapter_ids, request_slot_index):
    adapter = ((request_slot_index // SLOTS) * ADP_DEV + local_adapter_ids).astype(jnp.int32)
    base_part = jnp.dot(tokens, key_value_weight, preferred_element_type=jnp.float32)

    def one_request(packed):
        token_row, selected_part = packed
        down_matrix = lax.dynamic_index_in_dim(adapter_down_maps, selected_part, 0, keepdims=False)
        up_matrix = lax.dynamic_index_in_dim(adapter_up_maps, selected_part, 0, keepdims=False)
        low_rank = jnp.dot(token_row[None, :], down_matrix, preferred_element_type=jnp.float32).astype(jnp.bfloat16)
        key_part = jnp.dot(low_rank[:, :ADAPTER_RANK], up_matrix[:, :KEY_VALUE_WIDTH], preferred_element_type=jnp.float32)
        value_part = jnp.dot(low_rank[:, ADAPTER_RANK:], up_matrix[:, KEY_VALUE_WIDTH:], preferred_element_type=jnp.float32)
        return jnp.concatenate([key_part, value_part], axis=1)[0]

    adapted = lax.map(one_request, (tokens, adapter))
    return (base_part + adapted).astype(jnp.bfloat16)
```

```python
import functools

import jax
import jax.numpy as jnp
from jax import lax
from jax.experimental import pallas as pl
from jax.experimental.pallas import tpu as pltpu
from jax.sharding import PartitionSpec as P

SLOTS = 2
GROUP_ROWS = 64
LANES = 128
F32 = jnp.float32
BF16 = jnp.bfloat16
VMEM = pl.BlockSpec(memory_space=pltpu.VMEM)
HBM = pl.BlockSpec(memory_space=pl.ANY)
PARAMS = pltpu.CompilerParams(vmem_limit_bytes=48 * 1024 * 1024)


def contract(a, b, dim_a, dim_b):
    return lax.dot_general(a, b, (((dim_a,), (dim_b,)), ((), ())), preferred_element_type=F32)


def group_kernel(store_count, ids_ref, slots_ref, tokens_ref, *outs):
    place_ref, group_refs = outs[0], outs[1:]
    me = lax.axis_index("store")
    rows, width = tokens_ref.shape
    owner = slots_ref[...] // SLOTS
    relative = owner ^ me
    padded = max(8, store_count)
    mine = lax.broadcasted_iota(jnp.int32, (padded, rows), 0) == relative
    upto = lax.broadcasted_iota(jnp.int32, (rows, rows), 0) <= lax.broadcasted_iota(jnp.int32, (rows, rows), 1)
    count = contract(mine.astype(F32).astype(BF16), upto.astype(F32).astype(BF16), 1, 0)
    rank = jnp.sum(jnp.where(mine, count, 0.0), axis=0, keepdims=True).astype(jnp.int32) - 1
    tags = jnp.broadcast_to((ids_ref[...] + 1).astype(F32), (LANES, rows)).astype(BF16)
    position = lax.broadcasted_iota(jnp.int32, (GROUP_ROWS, rows), 0)
    for k, out in enumerate(group_refs):
        place = ((relative == k) & (rank == position)).astype(F32).astype(BF16)
        place_ref[k * GROUP_ROWS : (k + 1) * GROUP_ROWS, :] = place
        out[:, :width] = contract(place, tokens_ref[...], 1, 0).astype(BF16)
        out[:, width:] = contract(place, tags, 1, 1).astype(BF16)


def down_kernel(group_count, tensor_count, *refs):
    xs, down_ref = refs[:group_count], refs[group_count]
    tags_ref, pieces = refs[group_count + 1], refs[group_count + 2 : group_count + 2 + tensor_count]
    maps, low, low_t, sems = refs[group_count + 2 + tensor_count :]
    me = lax.axis_index("tensor")
    adapters, width, ranks = down_ref.shape
    copies, tops = [], []
    for g, x in enumerate(xs):
        tag = x[:, width:].astype(F32)
        top = jnp.max(tag)
        bottom = jnp.min(jnp.where(tag > 0, tag, top))
        tops.append(top)
        for slot, chosen in enumerate((bottom, top)):
            index = jnp.clip(chosen.astype(jnp.int32) - 1, 0, adapters - 1)
            copy = pltpu.make_async_copy(
                down_ref.at[index], maps.at[g, :, slot * ranks : (slot + 1) * ranks], sems.at[g, slot]
            )
            copy.start()
            copies.append(copy)
    for g, x in enumerate(xs):
        copies[2 * g].wait()
        copies[2 * g + 1].wait()
        both = contract(x[:, :width], maps[g], 1, 0)
        low[g * GROUP_ROWS : (g + 1) * GROUP_ROWS, :ranks] = jnp.where(
            x[:, width:].astype(F32) == tops[g], both[:, ranks:], both[:, :ranks]
        )
        low[g * GROUP_ROWS : (g + 1) * GROUP_ROWS, ranks:] = x[:, width:].astype(F32)
    low_t[...] = low[:, :ranks].T
    tags_ref[...] = low[:, ranks:].T[:8]
    portion = ranks // 2 // tensor_count
    for j, piece in enumerate(pieces):
        to = me ^ j
        for half in range(2):
            value = jnp.zeros((portion, low_t.shape[1]), F32)
            for b in range(tensor_count):
                start = half * (ranks // 2) + b * portion
                value = jnp.where(to == b, low_t[start : start + portion, :], value)
            piece[half * portion : (half + 1) * portion, :] = value


def base_kernel(group_count, *refs):
    xs, weight_ref, out_ref = refs[:group_count], refs[group_count], refs[group_count + 1]
    width = weight_ref.shape[0]
    for g, x in enumerate(xs):
        out_ref[g * GROUP_ROWS : (g + 1) * GROUP_ROWS, :] = contract(x[:, :width], weight_ref[...], 1, 0)


def up_kernel(group_count, tensor_count, adapters, base_ref, tags_ref, up_ref, *refs):
    pieces, outs, mixed = refs[:tensor_count], refs[tensor_count:-1], refs[-1]
    me = lax.axis_index("tensor")
    low = pieces[0][...]
    for piece in pieces[1:]:
        low = low + piece[...]
    low = low.astype(BF16).astype(F32)
    portion = low.shape[0] // 2
    tag = tags_ref[0:1, :]
    for half in range(2):
        part = low[half * portion : (half + 1) * portion, :]
        for a in range(adapters):
            mixed[half, a * portion : (a + 1) * portion, :] = jnp.where(tag == a + 1, part, 0.0)
    block = up_ref.shape[1] // tensor_count
    for j in range(tensor_count):
        to = me ^ j
        columns = pl.ds(pl.multiple_of(to * block, block), block)
        total = base_ref[:, columns] + contract(
            mixed[to // (tensor_count // 2)].astype(BF16), up_ref[:, columns], 0, 0
        )
        for g in range(group_count):
            outs[g * tensor_count + j][...] = total[g * GROUP_ROWS : (g + 1) * GROUP_ROWS, :].astype(BF16)


def finish_kernel(counts, place_ref, *refs):
    out_ref, grouped = refs[-2], refs[-1]
    first = 0
    for k, count in enumerate(counts):
        total = refs[first][...].astype(F32)
        for ref in refs[first + 1 : first + count]:
            total = total + ref[...].astype(F32)
        first += count
        grouped[k * GROUP_ROWS : (k + 1) * GROUP_ROWS, :] = total.astype(BF16)
    out_ref[...] = contract(place_ref[...], grouped[...], 0, 0).astype(BF16)


def shards(tokens, weight, down_maps, up_maps, local_ids, slot_index):
    store_count, tensor_count = lax.axis_size("store"), lax.axis_size("tensor")
    rows, width = tokens.shape
    adapters, _, ranks = down_maps.shape
    columns = weight.shape[1]
    portion = up_maps.shape[1]
    block = columns // tensor_count
    up_flat = up_maps.reshape(adapters * portion, columns)
    shape = jax.ShapeDtypeStruct

    def swap(value, k, j):
        pairs = [
            (s * tensor_count + t, (s ^ k) * tensor_count + (t ^ j))
            for s in range(store_count)
            for t in range(tensor_count)
        ]
        return lax.ppermute(value, ("store", "tensor"), pairs)

    place, *groups = pl.pallas_call(
        functools.partial(group_kernel, store_count),
        out_shape=[shape((store_count * GROUP_ROWS, rows), BF16)]
        + [shape((GROUP_ROWS, width + LANES), BF16)] * store_count,
        in_specs=[VMEM] * 3,
        out_specs=[VMEM] * (store_count + 1),
        compiler_params=PARAMS,
        name="group_rows",
    )(local_ids.reshape(1, rows), slot_index.reshape(1, rows), tokens)

    far = range(2, store_count)
    near = range(min(2, store_count))
    arrived = {}
    for k in far:
        arrived[k] = swap(groups[k], k, 0)
    for k in near:
        arrived[k] = swap(groups[k], k, 0) if k else groups[k]

    received = {}
    for part in (near, far):
        part = list(part)
        if not part:
            continue
        count = len(part)
        part_rows = count * GROUP_ROWS
        xs = [arrived[k] for k in part]
        tags, *pieces = pl.pallas_call(
            functools.partial(down_kernel, count, tensor_count),
            out_shape=[shape((8, part_rows), F32)] + [shape((2 * portion, part_rows), F32)] * tensor_count,
            in_specs=[VMEM] * count + [HBM],
            out_specs=[VMEM] * (tensor_count + 1),
            scratch_shapes=[
                pltpu.VMEM((count, width, 2 * ranks), BF16),
                pltpu.VMEM((part_rows, 2 * ranks), F32),
                pltpu.VMEM((ranks, part_rows), F32),
                pltpu.SemaphoreType.DMA((count, 2)),
            ],
            compiler_params=PARAMS,
            cost_estimate=pl.CostEstimate(
                flops=4 * part_rows * width * ranks, bytes_accessed=count * 4 * width * ranks, transcendentals=0
            ),
            name="low_products",
        )(*xs, down_maps)
        pieces = [swap(piece, 0, j) if j else piece for j, piece in enumerate(pieces)]
        step = 512 if columns % 512 == 0 else columns
        base = pl.pallas_call(
            functools.partial(base_kernel, count),
            grid=(columns // step,),
            out_shape=shape((part_rows, columns), F32),
            in_specs=[pl.BlockSpec((GROUP_ROWS, width + LANES), lambda i: (0, 0))] * count
            + [pl.BlockSpec((width, step), lambda i: (0, i))],
            out_specs=pl.BlockSpec((part_rows, step), lambda i: (0, i)),
            compiler_params=PARAMS,
            cost_estimate=pl.CostEstimate(
                flops=2 * part_rows * width * columns, bytes_accessed=2 * width * columns, transcendentals=0
            ),
            name="base_products",
        )(*xs, weight)
        shares = pl.pallas_call(
            functools.partial(up_kernel, count, tensor_count, adapters),
            out_shape=[shape((GROUP_ROWS, block), BF16)] * (count * tensor_count),
            in_specs=[VMEM] * (3 + tensor_count),
            out_specs=[VMEM] * (count * tensor_count),
            scratch_shapes=[pltpu.VMEM((2, adapters * portion, part_rows), F32)],
            compiler_params=PARAMS,
            name="up_products",
        )(base, tags, up_flat, *pieces)
        if store_count * tensor_count <= 16:
            for g, k in enumerate(part):
                received[k] = [
                    swap(shares[g * tensor_count + j], k, j) if k or j else shares[g * tensor_count + j]
                    for j in range(tensor_count)
                ]
        else:
            me = lax.axis_index("tensor")
            order = jnp.arange(tensor_count, dtype=jnp.int32) ^ me
            for g, k in enumerate(part):
                stacked = jnp.stack(shares[g * tensor_count : (g + 1) * tensor_count])
                stacked = jnp.take(stacked, order, axis=0)
                summed = lax.all_to_all(stacked, "tensor", 0, 0, tiled=True).astype(F32).sum(0).astype(BF16)
                received[k] = [swap(summed, k, 0) if k else summed]

    counts = tuple(len(received[k]) for k in range(store_count))
    return pl.pallas_call(
        functools.partial(finish_kernel, counts),
        out_shape=shape((rows, block), BF16),
        in_specs=[VMEM] * (1 + sum(counts)),
        out_specs=VMEM,
        scratch_shapes=[pltpu.VMEM((store_count * GROUP_ROWS, block), BF16)],
        compiler_params=PARAMS,
        name="finish",
    )(place, *[value for k in range(store_count) for value in received[k]])


def solution(mesh):
    in_specs = (
        P(("groups", "store"), "tensor"),
        P("tensor", None),
        P(("groups", "store"), "tensor", None),
        P(("groups", "store"), "tensor", None),
        P(("groups", "store")),
        P(("groups", "store")),
    )
    out_specs = P(("groups", "store"), "tensor")
    return jax.shard_map(shards, mesh=mesh, in_specs=in_specs, out_specs=out_specs, check_vma=False)
```

```python
import functools

import jax
import jax.numpy as jnp
from jax import lax
from jax.experimental import pallas as pl
from jax.experimental.pallas import tpu as pltpu
from jax.sharding import PartitionSpec as P

SLOTS = 2
GROUP_ROWS = 64
LANES = 128
F32 = jnp.float32
BF16 = jnp.bfloat16
VMEM = pl.BlockSpec(memory_space=pltpu.VMEM)
HBM = pl.BlockSpec(memory_space=pl.ANY)
PARAMS = pltpu.CompilerParams(vmem_limit_bytes=48 * 1024 * 1024)


def contract(a, b, dim_a, dim_b):
    return lax.dot_general(a, b, (((dim_a,), (dim_b,)), ((), ())), preferred_element_type=F32)


def group_kernel(store_count, ids_hbm, slots_hbm, tokens_hbm, *outs):
    place_ref, group_refs = outs[0], outs[1 : 1 + store_count]
    ids_ref, slots_ref, tokens_ref, sems = outs[1 + store_count :]
    me = lax.axis_index("store")
    copies = [
        pltpu.make_async_copy(source, target, sems.at[i])
        for i, (source, target) in enumerate(
            ((slots_hbm, slots_ref), (ids_hbm, ids_ref), (tokens_hbm, tokens_ref))
        )
    ]
    for copy in copies:
        copy.start()
    copies[0].wait()
    copies[1].wait()
    rows, width = tokens_ref.shape
    owner = slots_ref[...] // SLOTS
    relative = owner ^ me
    padded = max(8, store_count)
    mine = lax.broadcasted_iota(jnp.int32, (padded, rows), 0) == relative
    upto = lax.broadcasted_iota(jnp.int32, (rows, rows), 0) <= lax.broadcasted_iota(jnp.int32, (rows, rows), 1)
    count = contract(mine.astype(F32).astype(BF16), upto.astype(F32).astype(BF16), 1, 0)
    rank = jnp.sum(jnp.where(mine, count, 0.0), axis=0, keepdims=True).astype(jnp.int32) - 1
    tags = jnp.broadcast_to((ids_ref[...] + 1).astype(F32), (LANES, rows)).astype(BF16)
    position = lax.broadcasted_iota(jnp.int32, (GROUP_ROWS, rows), 0)
    places = []
    for k in range(store_count):
        place = ((relative == k) & (rank == position)).astype(F32).astype(BF16)
        place_ref[k * GROUP_ROWS : (k + 1) * GROUP_ROWS, :] = place
        places.append(place)
    copies[2].wait()
    for place, out in zip(places, group_refs):
        out[:, :width] = contract(place, tokens_ref[...], 1, 0).astype(BF16)
        out[:, width:] = contract(place, tags, 1, 1).astype(BF16)


def down_kernel(group_count, tensor_count, after_count, *refs):
    xs, down_ref, refs = refs[:group_count], refs[group_count], refs[group_count + 1 + after_count :]
    tags_ref, pieces = refs[0], refs[1 : 1 + tensor_count]
    maps, low, low_t, sems = refs[1 + tensor_count :]
    me = lax.axis_index("tensor")
    adapters, width, ranks = down_ref.shape
    copies, tops = [], []
    for g, x in enumerate(xs):
        tag = x[:, width:].astype(F32)
        top = jnp.max(tag)
        bottom = jnp.min(jnp.where(tag > 0, tag, top))
        tops.append(top)
        for slot, chosen in enumerate((bottom, top)):
            index = jnp.clip(chosen.astype(jnp.int32) - 1, 0, adapters - 1)
            copy = pltpu.make_async_copy(
                down_ref.at[index], maps.at[g, :, slot * ranks : (slot + 1) * ranks], sems.at[g, slot]
            )
            copy.start()
            copies.append(copy)
    for g, x in enumerate(xs):
        copies[2 * g].wait()
        copies[2 * g + 1].wait()
        both = contract(x[:, :width], maps[g], 1, 0)
        low[g * GROUP_ROWS : (g + 1) * GROUP_ROWS, :ranks] = jnp.where(
            x[:, width:].astype(F32) == tops[g], both[:, ranks:], both[:, :ranks]
        )
        low[g * GROUP_ROWS : (g + 1) * GROUP_ROWS, ranks:] = x[:, width:].astype(F32)
    low_t[...] = low[:, :ranks].T
    tags_ref[...] = low[:, ranks:].T[:8]
    portion = ranks // 2 // tensor_count
    for j, piece in enumerate(pieces):
        to = me ^ j
        for half in range(2):
            value = jnp.zeros((portion, low_t.shape[1]), F32)
            for b in range(tensor_count):
                start = half * (ranks // 2) + b * portion
                value = jnp.where(to == b, low_t[start : start + portion, :], value)
            piece[half * portion : (half + 1) * portion, :] = value


def base_kernel(group_count, *refs):
    xs, weight_ref, out_ref = refs[:group_count], refs[group_count], refs[group_count + 1]
    width = weight_ref.shape[0]
    x = jnp.concatenate([x[:, :width] for x in xs], axis=0)
    out_ref[...] = contract(x, weight_ref[...], 1, 0)


def up_kernel(group_count, tensor_count, adapters, base_ref, tags_ref, up_ref, *refs):
    pieces, outs, mixed = refs[:tensor_count], refs[tensor_count:-1], refs[-1]
    me = lax.axis_index("tensor")
    low = pieces[0][...]
    for piece in pieces[1:]:
        low = low + piece[...]
    low = low.astype(BF16).astype(F32)
    portion = low.shape[0] // 2
    tag = tags_ref[0:1, :]
    for half in range(2):
        part = low[half * portion : (half + 1) * portion, :]
        for a in range(adapters):
            mixed[half, a * portion : (a + 1) * portion, :] = jnp.where(tag == a + 1, part, 0.0)
    block = up_ref.shape[1] // tensor_count
    for j in range(tensor_count):
        to = me ^ j
        columns = pl.ds(pl.multiple_of(to * block, block), block)
        total = base_ref[:, columns] + contract(
            mixed[to // (tensor_count // 2)].astype(BF16), up_ref[:, columns], 0, 0
        )
        for p in range(len(outs) // tensor_count):
            out = outs[p * tensor_count + j]
            out[...] = total[p * out.shape[0] : (p + 1) * out.shape[0], :].astype(BF16)


def sum_kernel(counts, *refs):
    outs, first = refs[sum(counts) :], 0
    for p, count in enumerate(counts):
        for h, out in enumerate(outs):
            rows = pl.ds(h * GROUP_ROWS, GROUP_ROWS)
            total = refs[first][rows, :].astype(F32)
            for ref in refs[first + 1 : first + count]:
                total = total + ref[rows, :].astype(F32)
            out[p * GROUP_ROWS : (p + 1) * GROUP_ROWS, :] = total.astype(BF16)
        first += count


def finish_kernel(both, place_ref, *refs):
    halves, out_ref = refs[:both], refs[both]
    groups = []
    for k in range(place_ref.shape[0] // GROUP_ROWS):
        p = k // both
        groups.append(halves[k % both][p * GROUP_ROWS : (p + 1) * GROUP_ROWS, :])
    out_ref[...] = contract(place_ref[...], jnp.concatenate(groups, axis=0), 0, 0).astype(BF16)


def shards(tokens, weight, down_maps, up_maps, local_ids, slot_index):
    store_count, tensor_count = lax.axis_size("store"), lax.axis_size("tensor")
    rows, width = tokens.shape
    adapters, _, ranks = down_maps.shape
    columns = weight.shape[1]
    portion = up_maps.shape[1]
    block = columns // tensor_count
    up_flat = up_maps.reshape(adapters * portion, columns)
    shape = jax.ShapeDtypeStruct

    def swap(value, k, j):
        pairs = [
            (s * tensor_count + t, (s ^ k) * tensor_count + (t ^ j))
            for s in range(store_count)
            for t in range(tensor_count)
        ]
        return lax.ppermute(value, ("store", "tensor"), pairs)

    place, *groups = pl.pallas_call(
        functools.partial(group_kernel, store_count),
        out_shape=[shape((store_count * GROUP_ROWS, rows), BF16)]
        + [shape((GROUP_ROWS, width + LANES), BF16)] * store_count,
        in_specs=[HBM] * 3,
        out_specs=[VMEM] * (store_count + 1),
        scratch_shapes=[
            pltpu.VMEM((1, rows), jnp.int32),
            pltpu.VMEM((1, rows), jnp.int32),
            pltpu.VMEM((rows, width), BF16),
            pltpu.SemaphoreType.DMA((3,)),
        ],
        compiler_params=PARAMS,
        name="group_rows",
    )(local_ids.reshape(1, rows), slot_index.reshape(1, rows), tokens)

    both = min(2, store_count)
    far = range(2, store_count)
    near = range(both)
    arrived = {}
    for k in (*near, *far):
        arrived[k] = swap(groups[k], k, 0) if k else groups[k]

    received, after = [], []
    for part in (near, far):
        part = list(part)
        if not part:
            continue
        count = len(part)
        part_rows = count * GROUP_ROWS
        xs = [arrived[k] for k in part]
        tags, *pieces = pl.pallas_call(
            functools.partial(down_kernel, count, tensor_count, len(after)),
            out_shape=[shape((8, part_rows), F32)] + [shape((2 * portion, part_rows), F32)] * tensor_count,
            in_specs=[VMEM] * count + [HBM] * (1 + len(after)),
            out_specs=[VMEM] * (tensor_count + 1),
            scratch_shapes=[
                pltpu.VMEM((count, width, 2 * ranks), BF16),
                pltpu.VMEM((part_rows, 2 * ranks), F32),
                pltpu.VMEM((ranks, part_rows), F32),
                pltpu.SemaphoreType.DMA((count, 2)),
            ],
            compiler_params=PARAMS,
            cost_estimate=pl.CostEstimate(
                flops=4 * part_rows * width * ranks, bytes_accessed=count * 4 * width * ranks, transcendentals=0
            ),
            name="low_products",
        )(*xs, down_maps, *after)
        pieces = [swap(piece, 0, j) if j else piece for j, piece in enumerate(pieces)]
        step = 512 if columns % 512 == 0 else columns
        base = pl.pallas_call(
            functools.partial(base_kernel, count),
            grid=(columns // step,),
            out_shape=shape((part_rows, columns), F32),
            in_specs=[pl.BlockSpec((GROUP_ROWS, width + LANES), lambda i: (0, 0))] * count
            + [pl.BlockSpec((width, step), lambda i: (0, i))],
            out_specs=pl.BlockSpec((part_rows, step), lambda i: (0, i)),
            compiler_params=PARAMS,
            cost_estimate=pl.CostEstimate(
                flops=2 * part_rows * width * columns, bytes_accessed=2 * width * columns, transcendentals=0
            ),
            name="base_products",
        )(*xs, weight)
        shares = pl.pallas_call(
            functools.partial(up_kernel, count, tensor_count, adapters),
            out_shape=[shape((both * GROUP_ROWS, block), BF16)] * (count // both * tensor_count),
            in_specs=[VMEM] * (3 + tensor_count),
            out_specs=[VMEM] * (count // both * tensor_count),
            scratch_shapes=[pltpu.VMEM((2, adapters * portion, part_rows), F32)],
            compiler_params=PARAMS,
            name="up_products",
        )(base, tags, up_flat, *pieces)
        after = shares[:1]
        for p in range(count // both):
            k = part[p * both]
            mine = shares[p * tensor_count : (p + 1) * tensor_count]
            if store_count * tensor_count <= 16:
                received.append([swap(share, k, j) if k or j else share for j, share in enumerate(mine)])
            else:
                order = jnp.arange(tensor_count, dtype=jnp.int32) ^ lax.axis_index("tensor")
                stacked = jnp.take(jnp.stack(mine), order, axis=0)
                summed = lax.all_to_all(stacked, "tensor", 0, 0, tiled=True).astype(F32).sum(0).astype(BF16)
                received.append([swap(summed, k, 0) if k else summed])

    counts = tuple(len(blocks) for blocks in received)
    half_shape = shape((len(counts) * GROUP_ROWS, block), BF16)
    halves = pl.pallas_call(
        functools.partial(sum_kernel, counts),
        out_shape=[half_shape] * both,
        in_specs=[VMEM] * sum(counts),
        out_specs=[VMEM] * both,
        compiler_params=PARAMS,
        name="sums",
    )(*[value for blocks in received for value in blocks])
    if both == 2:
        halves = [halves[0], swap(halves[1], 1, 0)]
    return pl.pallas_call(
        functools.partial(finish_kernel, both),
        out_shape=shape((rows, block), BF16),
        in_specs=[VMEM] * (1 + both),
        out_specs=VMEM,
        compiler_params=PARAMS,
        name="finish",
    )(place, *halves)


def solution(mesh):
    in_specs = (
        P(("groups", "store"), "tensor"),
        P("tensor", None),
        P(("groups", "store"), "tensor", None),
        P(("groups", "store"), "tensor", None),
        P(("groups", "store")),
        P(("groups", "store")),
    )
    out_specs = P(("groups", "store"), "tensor")
    return jax.shard_map(shards, mesh=mesh, in_specs=in_specs, out_specs=out_specs, check_vma=False)
```

```python
import functools

import jax
import jax.numpy as jnp
from jax import lax
from jax.experimental import pallas as pl
from jax.experimental.pallas import tpu as pltpu
from jax.sharding import PartitionSpec as P

SLOTS = 2
GROUP_ROWS = 64
LANES = 128
F32 = jnp.float32
BF16 = jnp.bfloat16
VMEM = pl.BlockSpec(memory_space=pltpu.VMEM)
ANY = pl.BlockSpec(memory_space=pl.ANY)
PARAMS = pltpu.CompilerParams(vmem_limit_bytes=16 * 1024 * 1024)
WIDE = pltpu.CompilerParams(vmem_limit_bytes=48 * 1024 * 1024)
TWO_STEP_LOW = (False, False)
TWO_STEP_SHARES = (False, False)


def contract(a, b, dim_a, dim_b):
    return lax.dot_general(a, b, (((dim_a,), (dim_b,)), ((), ())), preferred_element_type=F32)


def group_kernel(store_count, adapters, codes_ref, tokens_ref, *outs):
    place_ref, group_refs = outs[0], outs[1:]
    me = lax.axis_index("store")
    rows, width = tokens_ref.shape
    codes = codes_ref[...]
    owner = codes // (SLOTS * adapters)
    relative = owner ^ me
    padded = max(8, store_count)
    mine = lax.broadcasted_iota(jnp.int32, (padded, rows), 0) == relative
    upto = lax.broadcasted_iota(jnp.int32, (rows, rows), 0) <= lax.broadcasted_iota(jnp.int32, (rows, rows), 1)
    count = contract(mine.astype(F32).astype(BF16), upto.astype(F32).astype(BF16), 1, 0)
    rank = jnp.sum(jnp.where(mine, count, 0.0), axis=0, keepdims=True).astype(jnp.int32) - 1
    tags = jnp.broadcast_to((codes % adapters + 1).astype(F32), (LANES, rows)).astype(BF16)
    position = lax.broadcasted_iota(jnp.int32, (GROUP_ROWS, rows), 0)
    places = []
    for k in range(store_count):
        place = ((relative == k) & (rank == position)).astype(F32).astype(BF16)
        place_ref[k * GROUP_ROWS : (k + 1) * GROUP_ROWS, :] = place
        places.append(place)
    for place, out in zip(places, group_refs):
        out[:, :width] = contract(place, tokens_ref[...], 1, 0).astype(BF16)
        out[:, width:] = contract(place, tags, 1, 1).astype(BF16)


def down_kernel(group_count, tensor_count, after_count, piece_count, *refs):
    xs, down_ref, refs = refs[:group_count], refs[group_count], refs[group_count + 1 + after_count :]
    tags_ref, pieces = refs[0], refs[1 : 1 + piece_count]
    low, low_t, *fetch = refs[1 + piece_count :]
    me = lax.axis_index("tensor")
    adapters, width, ranks = down_ref.shape
    chosen, copies = [], []
    for g, x in enumerate(xs):
        tag = x[:, width:].astype(F32)
        top = jnp.max(tag)
        bottom = jnp.min(jnp.where(tag > 0, tag, top))
        indices = [jnp.clip(value.astype(jnp.int32) - 1, 0, adapters - 1) for value in (bottom, top)]
        chosen.append((tag, top, indices))
        if fetch:
            for slot, index in enumerate(indices):
                copy = pltpu.make_async_copy(down_ref.at[index], fetch[0].at[g, slot], fetch[1].at[g, slot])
                copy.start()
                copies.append(copy)
    for g, x in enumerate(xs):
        tag, top, indices = chosen[g]
        if fetch:
            copies[2 * g].wait()
            copies[2 * g + 1].wait()
            maps = [fetch[0][g, slot] for slot in range(2)]
        else:
            maps = [down_ref[index] for index in indices]
        first, second = (contract(x[:, :width], value, 1, 0) for value in maps)
        low[g * GROUP_ROWS : (g + 1) * GROUP_ROWS, :ranks] = jnp.where(tag == top, second, first)
        low[g * GROUP_ROWS : (g + 1) * GROUP_ROWS, ranks:] = tag
    low_t[...] = low[:, :ranks].T
    tags_ref[...] = low[:, ranks:].T[:8]
    portion = ranks // 2 // tensor_count
    for j in range(tensor_count):
        out, place = pieces[j % piece_count], j // piece_count * 2 * portion
        to = me ^ j
        for half in range(2):
            value = jnp.zeros((portion, low_t.shape[1]), F32)
            for b in range(tensor_count):
                start = half * (ranks // 2) + b * portion
                value = jnp.where(to == b, low_t[start : start + portion, :], value)
            out[place + half * portion : place + (half + 1) * portion, :] = value


def fold_kernel(size, mine_ref, got_ref, keep_ref, send_ref):
    for i in range(mine_ref.shape[0] // size):
        out, rows = (keep_ref, send_ref)[i % 2], pl.ds(i * size, size)
        total = mine_ref[rows, :].astype(F32) + got_ref[rows, :].astype(F32)
        out[i // 2 * size : (i // 2 + 1) * size, :] = total.astype(out.dtype)


def fold(size, mine, got, keep_type):
    rows, columns = mine.shape
    return pl.pallas_call(
        functools.partial(fold_kernel, size),
        out_shape=[
            jax.ShapeDtypeStruct((rows // 2, columns), keep_type),
            jax.ShapeDtypeStruct((rows // 2, columns), got.dtype),
        ],
        in_specs=[VMEM] * 2,
        out_specs=[VMEM] * 2,
        compiler_params=PARAMS,
        name="fold",
    )(mine, got)


def base_kernel(group_count, *refs):
    xs, weight_ref, out_ref = refs[:group_count], refs[group_count], refs[group_count + 1]
    width = weight_ref.shape[0]
    x = jnp.concatenate([x[:, :width] for x in xs], axis=0)
    step = 512
    for i in range(out_ref.shape[1] // step):
        out_ref[:, i * step : (i + 1) * step] = contract(x, weight_ref[:, i * step : (i + 1) * step], 1, 0)


def up_kernel(tensor_count, adapters, piece_count, out_count, base_ref, tags_ref, up_ref, *refs):
    pieces, outs, mixed = refs[:piece_count], refs[piece_count:-1], refs[-1]
    me = lax.axis_index("tensor")
    low = pieces[0][...]
    for value in pieces[1:]:
        low = low + value[...]
    low = low.astype(BF16).astype(F32)
    portion = low.shape[0] // 2
    tag = tags_ref[0:1, :]
    for half in range(2):
        part = low[half * portion : (half + 1) * portion, :]
        for a in range(adapters):
            mixed[half, a * portion : (a + 1) * portion, :] = jnp.where(tag == a + 1, part, 0.0)
    block = up_ref.shape[1] // tensor_count
    for j in range(tensor_count):
        to = me ^ j
        columns = pl.ds(pl.multiple_of(to * block, block), block)
        total = base_ref[:, columns] + contract(
            mixed[to // (tensor_count // 2)].astype(BF16), up_ref[:, columns], 0, 0
        )
        rows = outs[0].shape[0] * out_count // tensor_count
        for p in range(len(outs) // out_count):
            out, place = outs[p * out_count + j % out_count], j // out_count * rows
            out[place : place + rows, :] = total[p * rows : (p + 1) * rows, :].astype(out.dtype)


def sum_kernel(counts, *refs):
    outs, first = refs[sum(counts) :], 0
    for p, count in enumerate(counts):
        for h, out in enumerate(outs):
            rows = pl.ds(h * GROUP_ROWS, GROUP_ROWS)
            total = refs[first][rows, :].astype(F32)
            for ref in refs[first + 1 : first + count]:
                total = total + ref[rows, :].astype(F32)
            out[p * GROUP_ROWS : (p + 1) * GROUP_ROWS, :] = total.astype(BF16)
        first += count


def finish_kernel(both, place_ref, *refs):
    halves, out_ref = refs[:both], refs[both]
    groups = []
    for k in range(place_ref.shape[0] // GROUP_ROWS):
        p = k // both
        groups.append(halves[k % both][p * GROUP_ROWS : (p + 1) * GROUP_ROWS, :])
    out_ref[...] = contract(place_ref[...], jnp.concatenate(groups, axis=0), 0, 0).astype(BF16)


def shards(tokens, weight, down_maps, up_maps, local_ids, slot_index):
    store_count, tensor_count = lax.axis_size("store"), lax.axis_size("tensor")
    rows, width = tokens.shape
    adapters, _, ranks = down_maps.shape
    columns = weight.shape[1]
    portion = up_maps.shape[1]
    block = columns // tensor_count
    up_flat = up_maps.reshape(adapters * portion, columns)
    shape = jax.ShapeDtypeStruct

    def swap(value, k, j):
        pairs = [
            (s * tensor_count + t, (s ^ k) * tensor_count + (t ^ j))
            for s in range(store_count)
            for t in range(tensor_count)
        ]
        return lax.ppermute(value, ("store", "tensor"), pairs)

    place, *groups = pl.pallas_call(
        functools.partial(group_kernel, store_count, adapters),
        out_shape=[shape((store_count * GROUP_ROWS, rows), BF16)]
        + [shape((GROUP_ROWS, width + LANES), BF16)] * store_count,
        in_specs=[VMEM] * 2,
        out_specs=[VMEM] * (store_count + 1),
        compiler_params=PARAMS,
        name="group_rows",
    )((slot_index * adapters + local_ids).reshape(1, rows), tokens)

    both = min(2, store_count)
    far = range(2, store_count)
    near = range(both)
    arrived = {}
    for k in (*near, *far):
        arrived[k] = swap(groups[k], k, 0) if k else groups[k]

    received, after = [], []
    for part in (near, far):
        part = list(part)
        if not part:
            continue
        count = len(part)
        part_rows = count * GROUP_ROWS
        xs = [arrived[k] for k in part]
        piece = 2 * portion
        two_step = tensor_count > 4 or TWO_STEP_LOW[bool(after)]
        piece_count = 2 if two_step else tensor_count
        tags, *pieces = pl.pallas_call(
            functools.partial(down_kernel, count, tensor_count, len(after), piece_count),
            out_shape=[shape((8, part_rows), F32)] + [shape((tensor_count // piece_count * piece, part_rows), F32)] * piece_count,
            in_specs=[VMEM] * count + [VMEM if after else ANY] + [ANY] * len(after),
            out_specs=[VMEM] * (1 + piece_count),
            scratch_shapes=[
                pltpu.VMEM((part_rows, 2 * ranks), F32),
                pltpu.VMEM((ranks, part_rows), F32),
            ]
            + ([] if after else [pltpu.VMEM((count, 2, width, ranks), BF16), pltpu.SemaphoreType.DMA((count, 2))]),
            compiler_params=PARAMS if after else WIDE,
            cost_estimate=pl.CostEstimate(
                flops=4 * part_rows * width * ranks, bytes_accessed=count * 4 * width * ranks, transcendentals=0
            ),
            name="low_products",
        )(*xs, down_maps, *after)
        if two_step:
            keep, send = pieces
            distance, got = 1, swap(send, 0, 1)
            while 2 * distance < tensor_count:
                distance *= 2
                keep, send = fold(piece, keep, got, F32)
                got = swap(send, 0, distance)
            pieces = [keep, got]
        else:
            pieces = [swap(value, 0, j) if j else value for j, value in enumerate(pieces)]
        base = pl.pallas_call(
            functools.partial(base_kernel, count),
            out_shape=shape((part_rows, columns), F32),
            in_specs=[VMEM] * (count + 1),
            out_specs=VMEM,
            compiler_params=PARAMS,
            cost_estimate=pl.CostEstimate(
                flops=2 * part_rows * width * columns, bytes_accessed=2 * width * columns, transcendentals=0
            ),
            name="base_products",
        )(*xs, weight)
        direct = store_count * tensor_count > 16 or not TWO_STEP_SHARES[bool(after)]
        out_count = tensor_count if direct else 2
        pair_rows = both * GROUP_ROWS
        shares = pl.pallas_call(
            functools.partial(up_kernel, tensor_count, adapters, len(pieces), out_count),
            out_shape=[
                shape((tensor_count // out_count * pair_rows, block), BF16 if direct or i % 2 else F32)
                for i in range(count // both * out_count)
            ],
            in_specs=[VMEM] * (3 + len(pieces)),
            out_specs=[VMEM] * (count // both * out_count),
            scratch_shapes=[pltpu.VMEM((2, adapters * portion, part_rows), F32)],
            compiler_params=PARAMS,
            name="up_products",
        )(base, tags, up_flat, *pieces)
        after = shares[-1:]
        for p in range(count // both):
            k = part[p * both]
            mine = shares[p * out_count : (p + 1) * out_count]
            if not direct:
                keep, send = mine
                distance, got = 1, swap(send, 0, 1)
                while 2 * distance < tensor_count:
                    distance *= 2
                    last = 2 * distance == tensor_count
                    keep, send = fold(pair_rows, keep, got, BF16 if k and last else F32)
                    got = swap(send, k if last else 0, distance)
                received.append([swap(keep, k, 0) if k else keep, got])
            elif store_count * tensor_count <= 16:
                blocks = [swap(mine[j], k, j) if k or j else mine[j] for j in reversed(range(tensor_count))]
                received.append(blocks[::-1])
            else:
                order = jnp.arange(tensor_count, dtype=jnp.int32) ^ lax.axis_index("tensor")
                stacked = jnp.take(jnp.stack(mine), order, axis=0)
                summed = lax.all_to_all(stacked, "tensor", 0, 0, tiled=True).astype(F32).sum(0).astype(BF16)
                received.append([swap(summed, k, 0) if k else summed])

    counts = tuple(len(blocks) for blocks in received)
    half_shape = shape((len(counts) * GROUP_ROWS, block), BF16)
    halves = pl.pallas_call(
        functools.partial(sum_kernel, counts),
        out_shape=[half_shape] * both,
        in_specs=[VMEM] * sum(counts),
        out_specs=[VMEM] * both,
        compiler_params=PARAMS,
        name="sums",
    )(*[value for blocks in received for value in blocks])
    if both == 2:
        halves = [halves[0], swap(halves[1], 1, 0)]
    return pl.pallas_call(
        functools.partial(finish_kernel, both),
        out_shape=shape((rows, block), BF16),
        in_specs=[VMEM] * (1 + both),
        out_specs=VMEM,
        compiler_params=PARAMS,
        name="finish",
    )(place, *halves)


def solution(mesh):
    in_specs = (
        P(("groups", "store"), "tensor"),
        P("tensor", None),
        P(("groups", "store"), "tensor", None),
        P(("groups", "store"), "tensor", None),
        P(("groups", "store")),
        P(("groups", "store")),
    )
    out_specs = P(("groups", "store"), "tensor")
    return jax.shard_map(shards, mesh=mesh, in_specs=in_specs, out_specs=out_specs, check_vma=False)
```

```python
import functools

import jax
import jax.numpy as jnp
from jax import lax
from jax.experimental import pallas as pl
from jax.experimental.pallas import tpu as pltpu
from jax.sharding import PartitionSpec as P

SLOTS = 2
GROUP_ROWS = 64
LANES = 128
F32 = jnp.float32
BF16 = jnp.bfloat16
VMEM = pl.BlockSpec(memory_space=pltpu.VMEM)
ANY = pl.BlockSpec(memory_space=pl.ANY)
PARAMS = pltpu.CompilerParams(vmem_limit_bytes=16 * 1024 * 1024)
WIDE = pltpu.CompilerParams(vmem_limit_bytes=48 * 1024 * 1024)
ORDER = ((3, 2, 1, 0), (0, 2, 3, 1))
LOW_ORDER = ((0, 2, 3, 1), (0, 1, 2, 3))
TWO_STEP_LOW = (False, False)
TWO_STEP_SHARES = (False, False)


def contract(a, b, dim_a, dim_b):
    return lax.dot_general(a, b, (((dim_a,), (dim_b,)), ((), ())), preferred_element_type=F32)


def group_kernel(store_count, adapters, codes_ref, tokens_ref, *outs):
    place_ref, group_refs = outs[0], outs[1:]
    me = lax.axis_index("store")
    rows, width = tokens_ref.shape
    codes = codes_ref[...]
    owner = codes // (SLOTS * adapters)
    relative = owner ^ me
    padded = max(8, store_count)
    mine = lax.broadcasted_iota(jnp.int32, (padded, rows), 0) == relative
    upto = lax.broadcasted_iota(jnp.int32, (rows, rows), 0) <= lax.broadcasted_iota(jnp.int32, (rows, rows), 1)
    count = contract(mine.astype(F32).astype(BF16), upto.astype(F32).astype(BF16), 1, 0)
    rank = jnp.sum(jnp.where(mine, count, 0.0), axis=0, keepdims=True).astype(jnp.int32) - 1
    tags = jnp.broadcast_to((codes % adapters + 1).astype(F32), (LANES, rows)).astype(BF16)
    position = lax.broadcasted_iota(jnp.int32, (GROUP_ROWS, rows), 0)
    places = []
    for k in range(store_count):
        place = ((relative == k) & (rank == position)).astype(F32).astype(BF16)
        place_ref[k * GROUP_ROWS : (k + 1) * GROUP_ROWS, :] = place
        places.append(place)
    for place, out in zip(places, group_refs):
        out[:, :width] = contract(place, tokens_ref[...], 1, 0).astype(BF16)
        out[:, width:] = contract(place, tags, 1, 1).astype(BF16)


def down_kernel(group_count, tensor_count, after_count, piece_count, *refs):
    xs, down_ref, refs = refs[:group_count], refs[group_count], refs[group_count + 1 + after_count :]
    tags_ref, pieces = refs[0], refs[1 : 1 + piece_count]
    low, low_t, *fetch = refs[1 + piece_count :]
    me = lax.axis_index("tensor")
    adapters, width, ranks = down_ref.shape
    chosen, copies = [], []
    for g, x in enumerate(xs):
        tag = x[:, width:].astype(F32)
        top = jnp.max(tag)
        bottom = jnp.min(jnp.where(tag > 0, tag, top))
        indices = [jnp.clip(value.astype(jnp.int32) - 1, 0, adapters - 1) for value in (bottom, top)]
        chosen.append((tag, top, indices))
        if fetch:
            for slot, index in enumerate(indices):
                copy = pltpu.make_async_copy(down_ref.at[index], fetch[0].at[g, slot], fetch[1].at[g, slot])
                copy.start()
                copies.append(copy)
    for g, x in enumerate(xs):
        tag, top, indices = chosen[g]
        if fetch:
            copies[2 * g].wait()
            copies[2 * g + 1].wait()
            maps = [fetch[0][g, slot] for slot in range(2)]
        else:
            maps = [down_ref[index] for index in indices]
        first, second = (contract(x[:, :width], value, 1, 0) for value in maps)
        low[g * GROUP_ROWS : (g + 1) * GROUP_ROWS, :ranks] = jnp.where(tag == top, second, first)
        low[g * GROUP_ROWS : (g + 1) * GROUP_ROWS, ranks:] = tag
    low_t[...] = low[:, :ranks].T
    tags_ref[...] = low[:, ranks:].T[:8]
    portion = ranks // 2 // tensor_count
    for j in range(tensor_count):
        out, place = pieces[j % piece_count], j // piece_count * 2 * portion
        to = me ^ j
        for half in range(2):
            value = jnp.zeros((portion, low_t.shape[1]), F32)
            for b in range(tensor_count):
                start = half * (ranks // 2) + b * portion
                value = jnp.where(to == b, low_t[start : start + portion, :], value)
            out[place + half * portion : place + (half + 1) * portion, :] = value


def fold_kernel(size, mine_ref, got_ref, keep_ref, send_ref):
    for i in range(mine_ref.shape[0] // size):
        out, rows = (keep_ref, send_ref)[i % 2], pl.ds(i * size, size)
        total = mine_ref[rows, :].astype(F32) + got_ref[rows, :].astype(F32)
        out[i // 2 * size : (i // 2 + 1) * size, :] = total.astype(out.dtype)


def fold(size, mine, got, keep_type):
    rows, columns = mine.shape
    return pl.pallas_call(
        functools.partial(fold_kernel, size),
        out_shape=[
            jax.ShapeDtypeStruct((rows // 2, columns), keep_type),
            jax.ShapeDtypeStruct((rows // 2, columns), got.dtype),
        ],
        in_specs=[VMEM] * 2,
        out_specs=[VMEM] * 2,
        compiler_params=PARAMS,
        name="fold",
    )(mine, got)


def base_kernel(group_count, *refs):
    xs, weight_ref, out_ref = refs[:group_count], refs[group_count], refs[group_count + 1]
    width = weight_ref.shape[0]
    x = jnp.concatenate([x[:, :width] for x in xs], axis=0)
    step = 512
    for i in range(out_ref.shape[1] // step):
        out_ref[:, i * step : (i + 1) * step] = contract(x, weight_ref[:, i * step : (i + 1) * step], 1, 0)


def up_kernel(tensor_count, adapters, piece_count, out_count, base_ref, tags_ref, up_ref, *refs):
    pieces, outs, mixed = refs[:piece_count], refs[piece_count:-1], refs[-1]
    me = lax.axis_index("tensor")
    low = pieces[0][...]
    for value in pieces[1:]:
        low = low + value[...]
    low = low.astype(BF16).astype(F32)
    portion = low.shape[0] // 2
    tag = tags_ref[0:1, :]
    for half in range(2):
        part = low[half * portion : (half + 1) * portion, :]
        for a in range(adapters):
            mixed[half, a * portion : (a + 1) * portion, :] = jnp.where(tag == a + 1, part, 0.0)
    block = up_ref.shape[1] // tensor_count
    for j in range(tensor_count):
        to = me ^ j
        columns = pl.ds(pl.multiple_of(to * block, block), block)
        total = base_ref[:, columns] + contract(
            mixed[to // (tensor_count // 2)].astype(BF16), up_ref[:, columns], 0, 0
        )
        rows = outs[0].shape[0] * out_count // tensor_count
        for p in range(len(outs) // out_count):
            out, place = outs[p * out_count + j % out_count], j // out_count * rows
            out[place : place + rows, :] = total[p * rows : (p + 1) * rows, :].astype(out.dtype)


def sum_kernel(counts, *refs):
    outs, first = refs[sum(counts) :], 0
    for p, count in enumerate(counts):
        for h, out in enumerate(outs):
            rows = pl.ds(h * GROUP_ROWS, GROUP_ROWS)
            total = refs[first][rows, :].astype(F32)
            for ref in refs[first + 1 : first + count]:
                total = total + ref[rows, :].astype(F32)
            out[p * GROUP_ROWS : (p + 1) * GROUP_ROWS, :] = total.astype(BF16)
        first += count


def finish_kernel(both, place_ref, *refs):
    halves, out_ref = refs[:both], refs[both]
    groups = []
    for k in range(place_ref.shape[0] // GROUP_ROWS):
        p = k // both
        groups.append(halves[k % both][p * GROUP_ROWS : (p + 1) * GROUP_ROWS, :])
    out_ref[...] = contract(place_ref[...], jnp.concatenate(groups, axis=0), 0, 0).astype(BF16)


def shards(tokens, weight, down_maps, up_maps, local_ids, slot_index):
    store_count, tensor_count = lax.axis_size("store"), lax.axis_size("tensor")
    rows, width = tokens.shape
    adapters, _, ranks = down_maps.shape
    columns = weight.shape[1]
    portion = up_maps.shape[1]
    block = columns // tensor_count
    up_flat = up_maps.reshape(adapters * portion, columns)
    shape = jax.ShapeDtypeStruct

    def swap(value, k, j):
        pairs = [
            (s * tensor_count + t, (s ^ k) * tensor_count + (t ^ j))
            for s in range(store_count)
            for t in range(tensor_count)
        ]
        return lax.ppermute(value, ("store", "tensor"), pairs)

    place, *groups = pl.pallas_call(
        functools.partial(group_kernel, store_count, adapters),
        out_shape=[shape((store_count * GROUP_ROWS, rows), BF16)]
        + [shape((GROUP_ROWS, width + LANES), BF16)] * store_count,
        in_specs=[VMEM] * 2,
        out_specs=[VMEM] * (store_count + 1),
        compiler_params=PARAMS,
        name="group_rows",
    )((slot_index * adapters + local_ids).reshape(1, rows), tokens)

    both = min(2, store_count)
    far = range(2, store_count)
    near = range(both)
    arrived = {}
    for k in (*near, *far):
        arrived[k] = swap(groups[k], k, 0) if k else groups[k]

    received, after = [], []
    for part in (near, far):
        part = list(part)
        if not part:
            continue
        count = len(part)
        part_rows = count * GROUP_ROWS
        xs = [arrived[k] for k in part]
        piece = 2 * portion
        two_step = tensor_count > 4 or TWO_STEP_LOW[bool(after)]
        piece_count = 2 if two_step else tensor_count
        tags, *pieces = pl.pallas_call(
            functools.partial(down_kernel, count, tensor_count, len(after), piece_count),
            out_shape=[shape((8, part_rows), F32)] + [shape((tensor_count // piece_count * piece, part_rows), F32)] * piece_count,
            in_specs=[VMEM] * count + [VMEM if after else ANY] + [ANY] * len(after),
            out_specs=[VMEM] * (1 + piece_count),
            scratch_shapes=[
                pltpu.VMEM((part_rows, 2 * ranks), F32),
                pltpu.VMEM((ranks, part_rows), F32),
            ]
            + ([] if after else [pltpu.VMEM((count, 2, width, ranks), BF16), pltpu.SemaphoreType.DMA((count, 2))]),
            compiler_params=PARAMS if after else WIDE,
            cost_estimate=pl.CostEstimate(
                flops=4 * part_rows * width * ranks, bytes_accessed=count * 4 * width * ranks, transcendentals=0
            ),
            name="low_products",
        )(*xs, down_maps, *after)
        if two_step:
            keep, send = pieces
            distance, got = 1, swap(send, 0, 1)
            while 2 * distance < tensor_count:
                distance *= 2
                keep, send = fold(piece, keep, got, F32)
                got = swap(send, 0, distance)
            pieces = [keep, got]
        else:
            order = LOW_ORDER[bool(after)] if tensor_count == 4 else range(tensor_count)
            pieces = [swap(pieces[j], 0, j) if j else pieces[j] for j in order]
        base = pl.pallas_call(
            functools.partial(base_kernel, count),
            out_shape=shape((part_rows, columns), F32),
            in_specs=[VMEM] * (count + 1),
            out_specs=VMEM,
            compiler_params=PARAMS,
            cost_estimate=pl.CostEstimate(
                flops=2 * part_rows * width * columns, bytes_accessed=2 * width * columns, transcendentals=0
            ),
            name="base_products",
        )(*xs, weight)
        direct = store_count * tensor_count > 16 or not TWO_STEP_SHARES[bool(after)]
        out_count = tensor_count if direct else 2
        pair_rows = both * GROUP_ROWS
        shares = pl.pallas_call(
            functools.partial(up_kernel, tensor_count, adapters, len(pieces), out_count),
            out_shape=[
                shape((tensor_count // out_count * pair_rows, block), BF16 if direct or i % 2 else F32)
                for i in range(count // both * out_count)
            ],
            in_specs=[VMEM] * (3 + len(pieces)),
            out_specs=[VMEM] * (count // both * out_count),
            scratch_shapes=[pltpu.VMEM((2, adapters * portion, part_rows), F32)],
            compiler_params=PARAMS,
            name="up_products",
        )(base, tags, up_flat, *pieces)
        after = shares[-1:]
        for p in range(count // both):
            k = part[p * both]
            mine = shares[p * out_count : (p + 1) * out_count]
            if not direct:
                keep, send = mine
                distance, got = 1, swap(send, 0, 1)
                while 2 * distance < tensor_count:
                    distance *= 2
                    last = 2 * distance == tensor_count
                    keep, send = fold(pair_rows, keep, got, BF16 if k and last else F32)
                    got = swap(send, k if last else 0, distance)
                received.append([swap(keep, k, 0) if k else keep, got])
            elif store_count * tensor_count <= 16:
                blocks = [swap(mine[j], k, j) if k or j else mine[j] for j in (ORDER[bool(k)] if tensor_count == 4 else range(tensor_count))]
                received.append(blocks)
            else:
                order = jnp.arange(tensor_count, dtype=jnp.int32) ^ lax.axis_index("tensor")
                stacked = jnp.take(jnp.stack(mine), order, axis=0)
                summed = lax.all_to_all(stacked, "tensor", 0, 0, tiled=True).astype(F32).sum(0).astype(BF16)
                received.append([swap(summed, k, 0) if k else summed])

    counts = tuple(len(blocks) for blocks in received)
    half_shape = shape((len(counts) * GROUP_ROWS, block), BF16)
    halves = pl.pallas_call(
        functools.partial(sum_kernel, counts),
        out_shape=[half_shape] * both,
        in_specs=[VMEM] * sum(counts),
        out_specs=[VMEM] * both,
        compiler_params=PARAMS,
        name="sums",
    )(*[value for blocks in received for value in blocks])
    if both == 2:
        halves = [halves[0], swap(halves[1], 1, 0)]
    return pl.pallas_call(
        functools.partial(finish_kernel, both),
        out_shape=shape((rows, block), BF16),
        in_specs=[VMEM] * (1 + both),
        out_specs=VMEM,
        compiler_params=PARAMS,
        name="finish",
    )(place, *halves)


def solution(mesh):
    in_specs = (
        P(("groups", "store"), "tensor"),
        P("tensor", None),
        P(("groups", "store"), "tensor", None),
        P(("groups", "store"), "tensor", None),
        P(("groups", "store")),
        P(("groups", "store")),
    )
    out_specs = P(("groups", "store"), "tensor")
    return jax.shard_map(shards, mesh=mesh, in_specs=in_specs, out_specs=out_specs, check_vma=False)
```
